32 devices in a mesh: energy: 8 (over y, x, core), layer: 4 (over z).
Axes of the slice: x: 2, y: 2, z: 4, core: 2. Of those that a mesh axis runs over, the one named last changes fastest.
Arguments:
- green_blocks: bfloat16 [32, 4, 2, 384, 384], P('energy', 'layer'), may hold values from -6 to 6
- offsets: int32 [4], replicated, may hold values from -4 to 4, as said below
- occupation: float32 [4], replicated, may hold values from 0.1 to 2
- coupling: int32 [4, 4], P('layer'), may hold values from 0 to 3
- vertex: bfloat16 [4, 2, 384, 384], replicated, may hold values from -0.15625 to 0.15625
- magnon_free: bfloat16 [4, 2, 384, 384], replicated, may hold values from -0.0068359375 to 0.0068359375
Outputs:
- sigma: bfloat16 [32, 4, 2, 384, 384], P('energy', 'layer')
The draws below stay inside these ranges and needn't reach their ends.
Inputs may be any that keep to these rules, and one draw needn't show every extreme that they name: `offsets`: each offset is a nonzero whole number; one equals 4 and one equals -4.
All inputs are finite; a program needn't handle non-finite values.
Results may differ from the reference program's by a relative error of at most 0.0056.
Values may be sent and summed in bfloat16 or wider, within the bound.
A program may use at most 192 MiB of HBM per device.

```python
import math
import jax
import jax.numpy as jnp
from jax import lax

NB = 384
NOFF = 4
NV = 4
E_DEV = 4
NE = 32
GROUPS = 4


def draw_offsets(key, part):
    first_key, second_key = jax.random.split(jax.random.fold_in(key, 11))
    raw = jax.random.randint(first_key, (NOFF - 2,), 0, 2 * E_DEV, dtype=jnp.int32)
    others = jnp.where(raw < E_DEV, raw - E_DEV, raw - E_DEV + 1).astype(jnp.int32)
    values = jnp.concatenate([jnp.array([E_DEV, -E_DEV], jnp.int32), others])
    order = jax.random.permutation(second_key, NOFF)
    return values[order].astype(jnp.int32)


def set_ends(result, own_key, low, high):
    shape = result.shape
    spot = [jax.random.randint(jax.random.fold_in(own_key, axis), (), 0, shape[axis]) for axis in range(len(shape))]
    result = result.at[tuple(spot)].set(low)
    longest = shape.index(max(shape))
    spot[longest] = (spot[longest] + 1) % shape[longest]
    return result.at[tuple(spot)].set(high)


def shard_levels(key, shape, cuts, low, top_value):
    gain = 1.0
    for axis_at, blocks in cuts:
        heights = jax.random.uniform(jax.random.fold_in(jax.random.fold_in(key, 6), axis_at), (blocks,), jnp.float32, low / len(cuts), top_value / len(cuts))
        gain = gain * jnp.repeat(jnp.exp(heights), shape[axis_at] // blocks).reshape((-1,) + (1,) * (len(shape) - 1 - axis_at))
    return gain


def normal_values(stream_key, extent, width, reach, shards=(), kind=jnp.bfloat16):
    drawn = jax.random.normal(stream_key, extent, jnp.float32) * width
    if len(shards) > 0:
        drawn = shard_levels(stream_key, extent, shards, -0.22, 0.18) * drawn
    return jnp.clip(drawn, min=-reach, max=reach).astype(kind)


def setup_inputs(seed: int = 0) -> dict:
    seeds = jax.random.split(jax.random.key(seed), 7)
    green_blocks = normal_values(seeds[0], (NE, GROUPS, 2, NB, NB), 1.0, 6.0, ((0, 8), (1, 4)))
    offsets = draw_offsets(jax.random.fold_in(seeds[6], 71), 0)
    occupation = jnp.clip(jnp.exp(jax.random.uniform(seeds[2], (NOFF,), jnp.float32, math.log(0.1), math.log(2.0))), 0.1, 2.0)
    coupling = set_ends(jax.random.randint(seeds[3], (GROUPS, NOFF), 0, NV), jax.random.fold_in(seeds[3], 1), 0, NV - 1).astype(jnp.int32)
    vertex = normal_values(seeds[4], (NV, 2, NB, NB), (4 * NB) ** -0.5, 0.15625)
    magnon_free = normal_values(seeds[5], (NOFF, 2, NB, NB), (16 * NB * NE * GROUPS) ** -0.5, 0.0068359375)
    return dict(green_blocks=green_blocks, offsets=offsets, occupation=occupation, coupling=coupling, vertex=vertex, magnon_free=magnon_free)


def complex_product(pattern, left_real, left_imag, right_real, right_imag):
    def product(first, second):
        return jnp.einsum(pattern, first.astype(jnp.float32), second.astype(jnp.float32))
    return (product(left_real, right_real) - product(left_imag, right_imag),
            product(left_real, right_imag) + product(left_imag, right_real))


def reference(green_blocks, offsets, occupation, coupling, vertex, magnon_free):
    margin = jnp.zeros((E_DEV,) + green_blocks.shape[1:], green_blocks.dtype)
    padded = jnp.concatenate([margin, green_blocks, margin], axis=0)
    chosen = vertex[coupling]
    weights = occupation[:, None, None, None, None]

    def partners(energy):
        below = jnp.take(padded, energy + E_DEV - offsets, axis=0)
        above = jnp.take(padded, energy + E_DEV + offsets, axis=0)
        return below.astype(jnp.float32), above.astype(jnp.float32)

    def accumulate(carry, energy):
        below, above = partners(energy)
        own = green_blocks[energy].astype(jnp.float32)
        flipped = jnp.swapaxes(above, -1, -2)
        real_part = jnp.sum(own[None, :, 0] * flipped[:, :, 0] - own[None, :, 1] * flipped[:, :, 1], axis=1)
        imag_part = jnp.sum(own[None, :, 0] * flipped[:, :, 1] + own[None, :, 1] * flipped[:, :, 0], axis=1)
        return carry + jnp.stack([real_part, imag_part], axis=1), None

    energies = jnp.arange(NE, dtype=jnp.int32)
    start = jnp.zeros((NOFF, 2, NB, NB), jnp.float32)
    polar, _ = lax.scan(accumulate, start, energies)
    polar = lax.optimization_barrier(polar.astype(jnp.bfloat16))
    magnon_real, magnon_imag = complex_product("kab,kbc->kac", polar[:, 0], polar[:, 1],
                                               magnon_free[:, 0], magnon_free[:, 1])
    magnon = lax.optimization_barrier(jnp.stack([magnon_real, magnon_imag], axis=1).astype(jnp.bfloat16))
    magnon = magnon.astype(jnp.float32)

    def sigma_at(energy):
        below, above = partners(energy)
        mixed = (weights * below + (weights + 1.0) * above).astype(jnp.bfloat16)
        mixed = lax.optimization_barrier(mixed)
        half_real, half_imag = complex_product("gkab,kgbc->kgac", chosen[:, :, 0], chosen[:, :, 1],
                                               mixed[:, :, 0], mixed[:, :, 1])
        half_real = lax.optimization_barrier(half_real.astype(jnp.bfloat16))
        half_imag = lax.optimization_barrier(half_imag.astype(jnp.bfloat16))
        born_real, born_imag = complex_product("kgab,gkcb->gac", half_real, half_imag,
                                               chosen[:, :, 0], -chosen[:, :, 1])
        summed = below + above
        hadamard_real = jnp.sum(magnon[:, 0][:, None] * summed[:, :, 0] - magnon[:, 1][:, None] * summed[:, :, 1], axis=0)
        hadamard_imag = jnp.sum(magnon[:, 0][:, None] * summed[:, :, 1] + magnon[:, 1][:, None] * summed[:, :, 0], axis=0)
        return jnp.stack([born_real + hadamard_real, born_imag + hadamard_imag], axis=1).astype(jnp.bfloat16)

    return lax.map(sigma_at, energies)
```

```python
import functools

import jax
import jax.numpy as jnp
from jax import lax
from jax.experimental import pallas as pl
from jax.experimental.pallas import tpu as pltpu
from jax.sharding import PartitionSpec as P

MESH = pl.DeviceIdType.MESH
F32 = jnp.float32
BF16 = jnp.bfloat16
ROWS = 32
ALIGN = 16


def reduction_plan(n_energy, n_layer, rows):
    bits = []
    bit = 2
    while bit < n_energy:
        bits.append(bit)
        bit *= 2
    kinds = [[1, 1]] if n_energy > 1 else []
    if bits:
        kinds.append([bits[-1], bits[0]])
    kinds.append([0, 0])
    for i in range(1, len(bits)):
        kinds.append([bits[-1 - i], bits[i]])
    plan = []
    size = rows
    for pair in kinds:
        parts = n_layer if pair[0] == 0 else 2
        if parts == 1:
            continue
        split = size % (parts * ALIGN) == 0
        after = size // parts if split else size
        plan.append((pair, parts, split, size, after))
        size = after
    return plan


def kernel(
    n_energy, n_layer, plan,
    off_ref, occ_ref, coup_ref, green_ref, vertex_ref, free_ref, out_ref,
    lo, up, own_t, wide, wide_t, acc, mix, half, part, full, mag, reach, coef, *rest,
):
    count = green_ref.shape[0]
    nb = green_ref.shape[-1]
    noff = off_ref.shape[0]
    nq = noff - 1
    stages = len(plan)
    landing = rest[:stages]
    halo_send, halo_recv = rest[stages], rest[stages + 1]
    sums_send = rest[stages + 2:2 * stages + 2]
    sums_recv = rest[2 * stages + 2:3 * stages + 2]
    spread_send = rest[3 * stages + 2:4 * stages + 2]
    spread_recv = rest[4 * stages + 2:5 * stages + 2]

    me = lax.axis_index("energy")
    layer = lax.axis_index("layer")

    barrier = pltpu.get_barrier_semaphore()

    def greet(energy, group):
        pl.semaphore_signal(barrier, inc=1, device_id=(energy, group), device_id_type=MESH)

    def flipped(bit):
        return me + bit * (1 - 2 * (lax.div(me, bit) % 2))

    peers = [(lax.rem(me + 1, n_energy), layer), (lax.rem(me + n_energy - 1, n_energy), layer)]
    for bit in sorted({b for pair, _, _, _, _ in plan for b in pair if b > 1}):
        peers.append((flipped(bit), layer))
    for r in range(1, n_layer):
        peers.append((me, lax.rem(layer + r, n_layer)))
    for peer in peers:
        greet(*peer)
    pl.semaphore_wait(barrier, len(peers))

    def send_next(e):
        return pltpu.make_async_remote_copy(
            src_ref=green_ref.at[e], dst_ref=lo.at[e], send_sem=halo_send.at[0, e],
            recv_sem=halo_recv.at[0, e], device_id=(me + 1, layer), device_id_type=MESH)

    def send_prev(e):
        return pltpu.make_async_remote_copy(
            src_ref=green_ref.at[e], dst_ref=up.at[count + e], send_sem=halo_send.at[1, e],
            recv_sem=halo_recv.at[1, e], device_id=(me - 1, layer), device_id_type=MESH)

    @pl.when(me > 0)
    def _():
        for e in range(count):
            send_prev(e).start()

    @pl.when(me < n_energy - 1)
    def _():
        for e in range(count):
            send_next(e).start()

    @pl.when(me == 0)
    def _():
        for e in range(count):
            lo[e] = jnp.zeros(lo.shape[1:], lo.dtype)

    @pl.when(me == n_energy - 1)
    def _():
        for e in range(count):
            up[count + e] = jnp.zeros(up.shape[1:], up.dtype)

    def stage_own(e, carry):
        block = green_ref[e]
        lo[count + e] = block
        up[e] = block
        own_t[e, 0] = block[0].T
        own_t[e, 1] = block[1].T
        return carry

    lax.fori_loop(0, count, stage_own, 0)

    offs = [off_ref[k] for k in range(noff)]

    def first_of(value):
        found = jnp.int32(noff - 1)
        for k in range(noff - 2, -1, -1):
            found = jnp.where(offs[k] == value, jnp.int32(k), found)
        return found

    low_slot, high_slot = first_of(-count), first_of(count)
    slots = [low_slot, high_slot]
    last = jnp.int32(-1)
    for _ in range(noff - 2):
        found = jnp.int32(noff - 1)
        for k in range(noff - 1, -1, -1):
            fits = jnp.logical_and(jnp.logical_and(k != low_slot, k != high_slot), k > last)
            found = jnp.where(fits, jnp.int32(k), found)
        slots.append(found)
        last = found
    positive = []
    for s, k in enumerate(slots):
        w = off_ref[k]
        n = occ_ref[k]
        sign = jnp.where(w > 0, jnp.float32(1.0), jnp.float32(0.0))
        positive.append(sign)
        reach[s] = jnp.where(w > 0, w, -w)
        coef[s] = n + 1.0 - sign
        coef[noff + s] = n + sign
        v = coup_ref[0, k]
        real, imag = vertex_ref[v, 0], vertex_ref[v, 1]
        wide[s, 0:nb, 0:nb] = real
        wide[s, 0:nb, nb:2 * nb] = -imag
        wide[s, nb:2 * nb, 0:nb] = imag
        wide[s, nb:2 * nb, nb:2 * nb] = real
        real_t, imag_t = real.T, imag.T
        wide_t[s, 0:nb, 0:nb] = real_t
        wide_t[s, 0:nb, nb:2 * nb] = -imag_t
        wide_t[s, nb:2 * nb, 0:nb] = imag_t
        wide_t[s, nb:2 * nb, nb:2 * nb] = real_t

    def clear(i, carry):
        acc[i] = jnp.zeros(acc.shape[1:], F32)
        return carry

    lax.fori_loop(0, acc.shape[0], clear, 0)

    def place(bit):
        return layer if bit == 0 else lax.div(me, bit) % 2

    def region(s, m):
        start = jnp.int32(0)
        for pair, parts, split, size, after in plan[:s]:
            if split:
                start = start + place(pair[m % 2]) * after
        return start

    def rows_at(start, size):
        return pl.ds(pl.multiple_of(start, ALIGN), size)

    def target(bit, r):
        return (me, lax.rem(layer + r, n_layer)) if bit == 0 else (flipped(bit), layer)

    def sum_copy(s, m, r):
        pair, parts, split, size, after = plan[s]
        bit = pair[m % 2]
        start = region(s, m)
        if split:
            mine = lax.rem(layer + r, n_layer) if bit == 0 else 1 - place(bit)
            start = start + mine * after
        return pltpu.make_async_remote_copy(
            src_ref=part.at[m, rows_at(start, after)], dst_ref=landing[s].at[m, r - 1],
            send_sem=sums_send[s].at[m, r - 1], recv_sem=sums_recv[s].at[m, r - 1],
            device_id=target(bit, r), device_id_type=MESH)

    def spread_copy(s, m, r):
        pair, parts, split, size, after = plan[s]
        where = rows_at(region(s + 1, m), after)
        return pltpu.make_async_remote_copy(
            src_ref=full.at[m, where], dst_ref=full.at[m, where],
            send_sem=spread_send[s].at[m, r - 1], recv_sem=spread_recv[s].at[m, r - 1],
            device_id=target(pair[m % 2], r), device_id_type=MESH)

    steps = [(sum_copy, s) for s in range(stages)]
    steps += [(spread_copy, s) for s in range(stages - 1, -1, -1) if plan[s][2]]

    def begin(i, m):
        make, s = steps[i]
        for r in range(1, plan[s][1]):
            make(s, m, r).start()

    def finish(i, m):
        make, s = steps[i]
        pair, parts, split, size, after = plan[s]
        for r in range(1, parts):
            make(s, m, r).wait()
        if make is sum_copy:
            where = rows_at(region(s + 1, m), after)
            total = part[m, where].astype(F32)
            for r in range(1, parts):
                total = total + landing[s][m, r - 1].astype(F32)
            if s == stages - 1:
                full[m, where] = total.astype(BF16)
            else:
                part[m, where] = total.astype(BF16)

    @pl.when(me < n_energy - 1)
    def _():
        for e in range(count):
            send_prev(e).wait_recv()

    for q in range(nq):
        w = reach[0] if q == 0 else reach[q + 1]

        def polar_rows(i, carry, q=q, w=w):
            rows = pl.ds(pl.multiple_of(i * ROWS, ROWS), ROWS)
            real = jnp.zeros((ROWS, nb), F32)
            imag = jnp.zeros((ROWS, nb), F32)
            for e in range(count):
                a_real = own_t[e, 0, rows].astype(F32)
                a_imag = own_t[e, 1, rows].astype(F32)
                b_real = up[e + w, 0, rows].astype(F32)
                b_imag = up[e + w, 1, rows].astype(F32)
                real = real + a_real * b_real - a_imag * b_imag
                imag = imag + a_real * b_imag + a_imag * b_real
            part[q, rows] = real.astype(BF16)
            part[q, pl.ds(pl.multiple_of(nb + i * ROWS, ROWS), ROWS)] = imag.astype(BF16)
            return carry

        lax.fori_loop(0, nb // ROWS, polar_rows, 0)
        begin(0, q)

    @pl.when(me > 0)
    def _():
        for e in range(count):
            send_next(e).wait_recv()

    pairs = count // 2
    units = noff * pairs

    def unit(i, carry):
        s, p = lax.div(i, pairs), lax.rem(i, pairs)
        w, c_low, c_up = reach[s], coef[s], coef[noff + s]
        for j in range(2):
            e = 2 * p + j
            for c in range(2):
                below = lo[count + e - w, c].astype(F32)
                above = up[e + w, c].astype(F32)
                mix[c * nb:(c + 1) * nb, j * nb:(j + 1) * nb] = (c_low * below + c_up * above).astype(BF16)
        product = jnp.dot(wide[s], mix[...], preferred_element_type=F32).astype(BF16)
        for j in range(2):
            for c in range(2):
                half[j * nb:(j + 1) * nb, c * nb:(c + 1) * nb] = product[c * nb:(c + 1) * nb, j * nb:(j + 1) * nb]
        acc[p] += jnp.dot(half[...], wide_t[s], preferred_element_type=F32)
        for step in range(min(len(steps), units)):
            @pl.when(i == step)
            def _(step=step):
                for m in range(nq):
                    finish(step, m)
                    if step + 1 < len(steps):
                        begin(step + 1, m)
        return carry

    lax.fori_loop(0, units, unit, 0)
    for step in range(units, len(steps)):
        for m in range(nq):
            finish(step, m)
            if step + 1 < len(steps):
                begin(step + 1, m)

    for s, k in enumerate(slots):
        f_real, f_imag = free_ref[k, 0], free_ref[k, 1]
        mix[0:nb, 0:nb] = f_real
        mix[0:nb, nb:2 * nb] = f_imag
        mix[nb:2 * nb, 0:nb] = -f_imag
        mix[nb:2 * nb, nb:2 * nb] = f_real
        q = 0 if s < 2 else s - 1
        for c in range(2):
            straight = full[q, c * nb:(c + 1) * nb]
            if s == 0:
                chosen = straight
            elif s == 1:
                chosen = straight.T
            else:
                turned = straight.T.astype(F32)
                chosen = (positive[s] * turned + (1.0 - positive[s]) * straight.astype(F32)).astype(BF16)
            half[0:nb, c * nb:(c + 1) * nb] = chosen
        magnon = jnp.dot(half[0:nb], mix[...], preferred_element_type=F32).astype(BF16).astype(F32)
        if s == 1:
            mag[0] += magnon
        else:
            mag[q] = magnon

    for e in range(count):
        def out_rows(i, carry, e=e):
            rows = pl.ds(pl.multiple_of(i * ROWS, ROWS), ROWS)
            base = pl.ds(pl.multiple_of((e % 2) * nb + i * ROWS, ROWS), ROWS)
            real = acc[e // 2, base, 0:nb]
            imag = acc[e // 2, base, nb:2 * nb]
            for q in range(nq):
                w = reach[0] if q == 0 else reach[q + 1]
                s_real = lo[count + e - w, 0, rows].astype(F32) + up[e + w, 0, rows].astype(F32)
                s_imag = lo[count + e - w, 1, rows].astype(F32) + up[e + w, 1, rows].astype(F32)
                m_real = mag[q, rows, 0:nb]
                m_imag = mag[q, rows, nb:2 * nb]
                real = real + m_real * s_real - m_imag * s_imag
                imag = imag + m_real * s_imag + m_imag * s_real
            out_ref[e, 0, 0, rows] = real.astype(BF16)
            out_ref[e, 0, 1, rows] = imag.astype(BF16)
            return carry

        lax.fori_loop(0, nb // ROWS, out_rows, 0)

    @pl.when(me > 0)
    def _():
        for e in range(count):
            send_prev(e).wait_send()

    @pl.when(me < n_energy - 1)
    def _():
        for e in range(count):
            send_next(e).wait_send()


def per_device(n_energy, n_layer, green_blocks, offsets, occupation, coupling, vertex, magnon_free):
    count, _, _, nb, _ = green_blocks.shape
    noff = offsets.shape[0]
    nq = noff - 1
    plan = reduction_plan(n_energy, n_layer, 2 * nb)
    smem = pl.BlockSpec(memory_space=pltpu.SMEM)
    vmem = pl.BlockSpec(memory_space=pltpu.VMEM)
    dma = pltpu.SemaphoreType.DMA
    scratch = [
        pltpu.VMEM((2 * count, 2, nb, nb), BF16),
        pltpu.VMEM((2 * count, 2, nb, nb), BF16),
        pltpu.VMEM((count, 2, nb, nb), BF16),
        pltpu.VMEM((noff, 2 * nb, 2 * nb), BF16),
        pltpu.VMEM((noff, 2 * nb, 2 * nb), BF16),
        pltpu.VMEM((count // 2, 2 * nb, 2 * nb), F32),
        pltpu.VMEM((2 * nb, 2 * nb), BF16),
        pltpu.VMEM((2 * nb, 2 * nb), BF16),
        pltpu.VMEM((nq, 2 * nb, nb), BF16),
        pltpu.VMEM((nq, 2 * nb, nb), BF16),
        pltpu.VMEM((nq, nb, 2 * nb), F32),
        pltpu.SMEM((noff,), jnp.int32),
        pltpu.SMEM((2 * noff,), F32),
    ]
    scratch += [pltpu.VMEM((nq, parts - 1, after, nb), BF16) for _, parts, _, _, after in plan]
    scratch += [dma((2, count)), dma((2, count))]
    for _ in range(4):
        scratch += [dma((nq, parts - 1)) for _, parts, _, _, _ in plan]
    flops = 16 * count * noff * 2 * nb ** 3
    return pl.pallas_call(
        functools.partial(kernel, n_energy, n_layer, plan),
        out_shape=jax.ShapeDtypeStruct(green_blocks.shape, BF16),
        in_specs=[smem, smem, smem, vmem, vmem, vmem],
        out_specs=vmem,
        scratch_shapes=scratch,
        compiler_params=pltpu.CompilerParams(
            collective_id=0, has_side_effects=True, vmem_limit_bytes=60 * 1024 * 1024),
        cost_estimate=pl.CostEstimate(
            flops=flops, bytes_accessed=4 * green_blocks.size * 2, transcendentals=0),
    )(offsets, occupation, coupling, green_blocks.reshape(count, 2, nb, nb), vertex, magnon_free)


def solution(mesh):
    placed = (P("energy", "layer", None, None, None), P(), P(), P("layer", None), P(), P())
    return jax.shard_map(
        functools.partial(per_device, mesh.shape["energy"], mesh.shape["layer"]),
        mesh=mesh,
        in_specs=placed,
        out_specs=P("energy", "layer", None, None, None),
        check_vma=False,
    )
```

```python
import functools

import jax
import jax.numpy as jnp
from jax import lax
from jax.experimental import pallas as pl
from jax.experimental.pallas import tpu as pltpu
from jax.sharding import PartitionSpec as P

MESH = pl.DeviceIdType.MESH
F32 = jnp.float32
BF16 = jnp.bfloat16
ROWS = 32
AHEAD = 3
ALIGN = 16


def reduction_plan(n_energy, n_layer, rows):
    bits = []
    bit = 2
    while bit < n_energy:
        bits.append(bit)
        bit *= 2
    kinds = [[1, 1]] if n_energy > 1 else []
    if bits:
        kinds.append([bits[-1], bits[-1]])
    kinds.append([0, 0])
    for i in range(1, len(bits)):
        kinds.append([bits[-1 - i], bits[-1 - i]])
    plan = []
    size = rows
    for pair in kinds:
        parts = n_layer if pair[0] == 0 else 2
        if parts == 1:
            continue
        split = size % (parts * ALIGN) == 0
        after = size // parts if split else size
        plan.append((pair, parts, split, size, after))
        size = after
    return plan


def kernel(
    n_energy, n_layer, plan,
    off_ref, occ_ref, coup_ref, green_ref, vertex_ref, free_ref, out_ref,
    lo, up, turned, wide, wide_t, acc, mix, half, part, full, mag, reach, coef, *rest,
):
    count = green_ref.shape[0]
    nb = green_ref.shape[-1]
    noff = off_ref.shape[0]
    nq = noff - 1
    stages = len(plan)
    landing = rest[:stages]
    halo_send, halo_recv = rest[stages], rest[stages + 1]
    sums_send = rest[stages + 2:2 * stages + 2]
    sums_recv = rest[2 * stages + 2:3 * stages + 2]
    spread_send = rest[3 * stages + 2:4 * stages + 2]
    spread_recv = rest[4 * stages + 2:5 * stages + 2]

    me = lax.axis_index("energy")
    layer = lax.axis_index("layer")

    barrier = pltpu.get_barrier_semaphore()

    def greet(energy, group):
        pl.semaphore_signal(barrier, inc=1, device_id=(energy, group), device_id_type=MESH)

    def flipped(bit):
        return me + bit * (1 - 2 * (lax.div(me, bit) % 2))

    peers = [(lax.rem(me + 1, n_energy), layer), (lax.rem(me + n_energy - 1, n_energy), layer)]
    for bit in sorted({b for pair, _, _, _, _ in plan for b in pair if b > 1}):
        peers.append((flipped(bit), layer))
    for r in range(1, n_layer):
        peers.append((me, lax.rem(layer + r, n_layer)))
    for peer in peers:
        greet(*peer)
    pl.semaphore_wait(barrier, len(peers))

    def send_next(e):
        return pltpu.make_async_remote_copy(
            src_ref=green_ref.at[e], dst_ref=lo.at[e], send_sem=halo_send.at[0, e],
            recv_sem=halo_recv.at[0, e], device_id=(me + 1, layer), device_id_type=MESH)

    def send_prev(e):
        return pltpu.make_async_remote_copy(
            src_ref=green_ref.at[e], dst_ref=up.at[count + e], send_sem=halo_send.at[1, e],
            recv_sem=halo_recv.at[1, e], device_id=(me - 1, layer), device_id_type=MESH)

    early = count // 2
    prev_order = [list(range(early)), list(range(early, count))]
    next_order = [list(range(early, count)), list(range(early))]

    def halo(part_of, act):
        @pl.when(me > 0)
        def _():
            for e in prev_order[part_of]:
                getattr(send_prev(e), act)()

        @pl.when(me < n_energy - 1)
        def _():
            for e in next_order[part_of]:
                getattr(send_next(e), act)()

    def halo_arrived(part_of):
        @pl.when(me < n_energy - 1)
        def _():
            for e in prev_order[part_of]:
                send_prev(e).wait_recv()

        @pl.when(me > 0)
        def _():
            for e in next_order[part_of]:
                send_next(e).wait_recv()

    halo(0, "start")

    @pl.when(me == 0)
    def _():
        for e in range(count):
            lo[e] = jnp.zeros(lo.shape[1:], lo.dtype)

    @pl.when(me == n_energy - 1)
    def _():
        for e in range(count):
            up[count + e] = jnp.zeros(up.shape[1:], up.dtype)

    def stage_own(e, carry):
        block = green_ref[e]
        lo[count + e] = block
        up[e] = block
        turned[count - early + e, 0] = block[0].T
        turned[count - early + e, 1] = block[1].T
        return carry

    lax.fori_loop(0, count, stage_own, 0)

    offs = [off_ref[k] for k in range(noff)]

    def first_of(value):
        found = jnp.int32(noff - 1)
        for k in range(noff - 2, -1, -1):
            found = jnp.where(offs[k] == value, jnp.int32(k), found)
        return found

    low_slot, high_slot = first_of(-count), first_of(count)
    slots = [low_slot, high_slot]
    last = jnp.int32(-1)
    for _ in range(noff - 2):
        found = jnp.int32(noff - 1)
        for k in range(noff - 1, -1, -1):
            fits = jnp.logical_and(jnp.logical_and(k != low_slot, k != high_slot), k > last)
            found = jnp.where(fits, jnp.int32(k), found)
        slots.append(found)
        last = found
    positive = []
    for s, k in enumerate(slots):
        w = off_ref[k]
        n = occ_ref[k]
        sign = jnp.where(w > 0, jnp.float32(1.0), jnp.float32(0.0))
        positive.append(sign)
        reach[s] = jnp.clip(jnp.where(w > 0, w, -w), 1, count)
        coef[s] = n + 1.0 - sign
        coef[noff + s] = n + sign
        v = coup_ref[0, k]
        real, imag = vertex_ref[v, 0], vertex_ref[v, 1]
        wide[s, 0:nb, 0:nb] = real
        wide[s, 0:nb, nb:2 * nb] = -imag
        wide[s, nb:2 * nb, 0:nb] = imag
        wide[s, nb:2 * nb, nb:2 * nb] = real
        real_t, imag_t = real.T, imag.T
        wide_t[s, 0:nb, 0:nb] = real_t
        wide_t[s, 0:nb, nb:2 * nb] = -imag_t
        wide_t[s, nb:2 * nb, 0:nb] = imag_t
        wide_t[s, nb:2 * nb, nb:2 * nb] = real_t

    def clear(i, carry):
        acc[i] = jnp.zeros(acc.shape[1:], F32)
        return carry

    lax.fori_loop(0, acc.shape[0], clear, 0)

    def place(bit):
        return layer if bit == 0 else lax.div(me, bit) % 2

    def region(s, m):
        start = jnp.int32(0)
        for pair, parts, split, size, after in plan[:s]:
            if split:
                start = start + place(pair[m % 2]) * after
        return start

    def rows_at(start, size):
        return pl.ds(pl.multiple_of(start, ALIGN), size)

    def target(bit, r):
        return (me, lax.rem(layer + r, n_layer)) if bit == 0 else (flipped(bit), layer)

    def sum_copy(s, m, r):
        pair, parts, split, size, after = plan[s]
        bit = pair[m % 2]
        start = region(s, m)
        if split:
            mine = lax.rem(layer + r, n_layer) if bit == 0 else 1 - place(bit)
            start = start + mine * after
        return pltpu.make_async_remote_copy(
            src_ref=part.at[m, rows_at(start, after)], dst_ref=landing[s].at[m, r - 1],
            send_sem=sums_send[s].at[m, r - 1], recv_sem=sums_recv[s].at[m, r - 1],
            device_id=target(bit, r), device_id_type=MESH)

    def spread_copy(s, m, r):
        pair, parts, split, size, after = plan[s]
        where = rows_at(region(s + 1, m), after)
        return pltpu.make_async_remote_copy(
            src_ref=full.at[m, where], dst_ref=full.at[m, where],
            send_sem=spread_send[s].at[m, r - 1], recv_sem=spread_recv[s].at[m, r - 1],
            device_id=target(pair[m % 2], r), device_id_type=MESH)

    steps = [(sum_copy, s) for s in range(stages)]
    steps += [(spread_copy, s) for s in range(stages - 1, -1, -1) if plan[s][2]]

    def begin(i, m):
        make, s = steps[i]
        for r in range(1, plan[s][1]):
            make(s, m, r).start()

    def finish(i, m):
        make, s = steps[i]
        pair, parts, split, size, after = plan[s]
        for r in range(1, parts):
            make(s, m, r).wait()
        if make is sum_copy:
            where = rows_at(region(s + 1, m), after)
            total = part[m, where].astype(F32)
            for r in range(1, parts):
                total = total + landing[s][m, r - 1].astype(F32)
            if s == stages - 1:
                full[m, where] = total.astype(BF16)
            else:
                part[m, where] = total.astype(BF16)

    halo(0, "wait_send")
    halo(1, "start")
    halo_arrived(0)
    for i in range(count - early):
        turned[i, 0] = lo[early + i, 0].T
        turned[i, 1] = lo[early + i, 1].T

    for q in range(nq):
        w = count if q == 0 else reach[q + 1]

        def polar_rows(i, carry, q=q, w=w):
            rows = pl.ds(pl.multiple_of(i * ROWS, ROWS), ROWS)
            real = jnp.zeros((ROWS, nb), F32)
            imag = jnp.zeros((ROWS, nb), F32)
            for f in range(early, count + early):
                b_real, b_imag = up[f, 0, rows], up[f, 1, rows]
                at = count - early + f - w
                if f > count and q > 0:
                    inside = w <= f - count
                    b_real = jnp.where(inside, up[f - count, 0, rows].astype(F32), b_real.astype(F32))
                    b_imag = jnp.where(inside, up[f - count, 1, rows].astype(F32), b_imag.astype(F32))
                    at = jnp.where(inside, at - count, at)
                b_real, b_imag = b_real.astype(F32), b_imag.astype(F32)
                a_real = turned[at, 0, rows].astype(F32)
                a_imag = turned[at, 1, rows].astype(F32)
                real = real + a_real * b_real - a_imag * b_imag
                imag = imag + a_real * b_imag + a_imag * b_real
            part[q, rows] = real.astype(BF16)
            part[q, pl.ds(pl.multiple_of(nb + i * ROWS, ROWS), ROWS)] = imag.astype(BF16)
            return carry

        lax.fori_loop(0, nb // ROWS, polar_rows, 0)
        begin(0, q)

    def advance(step):
        for m in range(nq):
            finish(step, m)
            if step + 1 < len(steps):
                begin(step + 1, m)

    ahead = min(AHEAD, len(steps))
    for step in range(ahead):
        advance(step)
    halo_arrived(1)

    pairs = count // 2
    units = noff * pairs

    def unit(i, carry):
        s, p = lax.div(i, pairs), lax.rem(i, pairs)
        w, c_low, c_up = reach[s], coef[s], coef[noff + s]
        for j in range(2):
            e = 2 * p + j
            for c in range(2):
                below = lo[count + e - w, c].astype(F32)
                above = up[e + w, c].astype(F32)
                mix[c * nb:(c + 1) * nb, j * nb:(j + 1) * nb] = (c_low * below + c_up * above).astype(BF16)
        product = jnp.dot(wide[s], mix[...], preferred_element_type=F32).astype(BF16)
        for j in range(2):
            for c in range(2):
                half[j * nb:(j + 1) * nb, c * nb:(c + 1) * nb] = product[c * nb:(c + 1) * nb, j * nb:(j + 1) * nb]
        acc[p] += jnp.dot(half[...], wide_t[s], preferred_element_type=F32)
        for step in range(ahead, min(len(steps), ahead + units)):
            @pl.when(i == step - ahead)
            def _(step=step):
                advance(step)
        return carry

    lax.fori_loop(0, units, unit, 0)
    for step in range(ahead + units, len(steps)):
        advance(step)

    for s, k in enumerate(slots):
        f_real, f_imag = free_ref[k, 0], free_ref[k, 1]
        mix[0:nb, 0:nb] = f_real
        mix[0:nb, nb:2 * nb] = f_imag
        mix[nb:2 * nb, 0:nb] = -f_imag
        mix[nb:2 * nb, nb:2 * nb] = f_real
        q = 0 if s < 2 else s - 1
        for c in range(2):
            straight = full[q, c * nb:(c + 1) * nb]
            if s == 0:
                chosen = straight
            elif s == 1:
                chosen = straight.T
            else:
                flip = straight.T.astype(F32)
                chosen = (positive[s] * flip + (1.0 - positive[s]) * straight.astype(F32)).astype(BF16)
            half[0:nb, c * nb:(c + 1) * nb] = chosen
        magnon = jnp.dot(half[0:nb], mix[...], preferred_element_type=F32).astype(BF16).astype(F32)
        if s == 1:
            mag[0] += magnon
        else:
            mag[q] = magnon

    for e in range(count):
        def out_rows(i, carry, e=e):
            rows = pl.ds(pl.multiple_of(i * ROWS, ROWS), ROWS)
            base = pl.ds(pl.multiple_of((e % 2) * nb + i * ROWS, ROWS), ROWS)
            real = acc[e // 2, base, 0:nb]
            imag = acc[e // 2, base, nb:2 * nb]
            for q in range(nq):
                w = reach[0] if q == 0 else reach[q + 1]
                s_real = lo[count + e - w, 0, rows].astype(F32) + up[e + w, 0, rows].astype(F32)
                s_imag = lo[count + e - w, 1, rows].astype(F32) + up[e + w, 1, rows].astype(F32)
                m_real = mag[q, rows, 0:nb]
                m_imag = mag[q, rows, nb:2 * nb]
                real = real + m_real * s_real - m_imag * s_imag
                imag = imag + m_real * s_imag + m_imag * s_real
            out_ref[e, 0, 0, rows] = real.astype(BF16)
            out_ref[e, 0, 1, rows] = imag.astype(BF16)
            return carry

        lax.fori_loop(0, nb // ROWS, out_rows, 0)

    halo(1, "wait_send")


def per_device(n_energy, n_layer, green_blocks, offsets, occupation, coupling, vertex, magnon_free):
    count, _, _, nb, _ = green_blocks.shape
    noff = offsets.shape[0]
    nq = noff - 1
    plan = reduction_plan(n_energy, n_layer, 2 * nb)
    smem = pl.BlockSpec(memory_space=pltpu.SMEM)
    vmem = pl.BlockSpec(memory_space=pltpu.VMEM)
    dma = pltpu.SemaphoreType.DMA
    scratch = [
        pltpu.VMEM((2 * count, 2, nb, nb), BF16),
        pltpu.VMEM((2 * count, 2, nb, nb), BF16),
        pltpu.VMEM((2 * count - count // 2, 2, nb, nb), BF16),
        pltpu.VMEM((noff, 2 * nb, 2 * nb), BF16),
        pltpu.VMEM((noff, 2 * nb, 2 * nb), BF16),
        pltpu.VMEM((count // 2, 2 * nb, 2 * nb), F32),
        pltpu.VMEM((2 * nb, 2 * nb), BF16),
        pltpu.VMEM((2 * nb, 2 * nb), BF16),
        pltpu.VMEM((nq, 2 * nb, nb), BF16),
        pltpu.VMEM((nq, 2 * nb, nb), BF16),
        pltpu.VMEM((nq, nb, 2 * nb), F32),
        pltpu.SMEM((noff,), jnp.int32),
        pltpu.SMEM((2 * noff,), F32),
    ]
    scratch += [pltpu.VMEM((nq, parts - 1, after, nb), BF16) for _, parts, _, _, after in plan]
    scratch += [dma((2, count)), dma((2, count))]
    for _ in range(4):
        scratch += [dma((nq, parts - 1)) for _, parts, _, _, _ in plan]
    flops = 16 * count * noff * 2 * nb ** 3
    return pl.pallas_call(
        functools.partial(kernel, n_energy, n_layer, plan),
        out_shape=jax.ShapeDtypeStruct(green_blocks.shape, BF16),
        in_specs=[smem, smem, smem, vmem, vmem, vmem],
        out_specs=vmem,
        scratch_shapes=scratch,
        compiler_params=pltpu.CompilerParams(
            collective_id=0, has_side_effects=True, vmem_limit_bytes=60 * 1024 * 1024),
        cost_estimate=pl.CostEstimate(
            flops=flops, bytes_accessed=4 * green_blocks.size * 2, transcendentals=0),
    )(offsets, occupation, coupling, green_blocks.reshape(count, 2, nb, nb), vertex, magnon_free)


def solution(mesh):
    placed = (P("energy", "layer", None, None, None), P(), P(), P("layer", None), P(), P())
    return jax.shard_map(
        functools.partial(per_device, mesh.shape["energy"], mesh.shape["layer"]),
        mesh=mesh,
        in_specs=placed,
        out_specs=P("energy", "layer", None, None, None),
        check_vma=False,
    )
```

```python
import functools

import jax
import jax.numpy as jnp
from jax import lax
from jax.experimental import pallas as pl
from jax.experimental.pallas import tpu as pltpu
from jax.sharding import PartitionSpec as P

MESH = pl.DeviceIdType.MESH
F32 = jnp.float32
BF16 = jnp.bfloat16
ROWS = 32
AHEAD = 3
LANES = 128
WIDTH = 256
ALIGN = 16


def reduction_plan(n_energy, n_layer, rows):
    bits = []
    bit = 2
    while bit < n_energy:
        bits.append(bit)
        bit *= 2
    kinds = [[1, 1]] if n_energy > 1 else []
    if bits:
        kinds.append([bits[-1], bits[-1]])
    kinds.append([0, 0])
    for i in range(1, len(bits)):
        kinds.append([bits[-1 - i], bits[-1 - i]])
    plan = []
    size = rows
    for pair in kinds:
        parts = n_layer if pair[0] == 0 else 2
        if parts == 1:
            continue
        split = size % (parts * ALIGN) == 0
        after = size // parts if split else size
        plan.append((pair, parts, split, size, after))
        size = after
    return plan


def kernel(
    n_energy, n_layer, plan,
    off_ref, occ_ref, coup_ref, green_ref, vertex_ref, free_ref, out_ref,
    lo, up, turned, wide, wide_t, acc, mix, half, part, full, mag, reach, coef, *rest,
):
    count = green_ref.shape[0]
    nb = green_ref.shape[-1]
    noff = off_ref.shape[0]
    nq = noff - 1
    stages = len(plan)
    landing = rest[:stages]
    halo_send, halo_recv = rest[stages], rest[stages + 1]
    sums_send = rest[stages + 2:2 * stages + 2]
    sums_recv = rest[2 * stages + 2:3 * stages + 2]
    spread_send = rest[3 * stages + 2:4 * stages + 2]
    spread_recv = rest[4 * stages + 2:5 * stages + 2]

    me = lax.axis_index("energy")
    layer = lax.axis_index("layer")

    barrier = pltpu.get_barrier_semaphore()

    def greet(energy, group):
        pl.semaphore_signal(barrier, inc=1, device_id=(energy, group), device_id_type=MESH)

    def flipped(bit):
        return me + bit * (1 - 2 * (lax.div(me, bit) % 2))

    peers = [(lax.rem(me + 1, n_energy), layer), (lax.rem(me + n_energy - 1, n_energy), layer)]
    for bit in sorted({b for pair, _, _, _, _ in plan for b in pair if b > 1}):
        peers.append((flipped(bit), layer))
    for r in range(1, n_layer):
        peers.append((me, lax.rem(layer + r, n_layer)))
    for peer in peers:
        greet(*peer)
    pl.semaphore_wait(barrier, len(peers))

    def send_next(e):
        return pltpu.make_async_remote_copy(
            src_ref=green_ref.at[e], dst_ref=lo.at[e], send_sem=halo_send.at[0, e],
            recv_sem=halo_recv.at[0, e], device_id=(me + 1, layer), device_id_type=MESH)

    def send_prev(e):
        return pltpu.make_async_remote_copy(
            src_ref=green_ref.at[e], dst_ref=up.at[count + e], send_sem=halo_send.at[1, e],
            recv_sem=halo_recv.at[1, e], device_id=(me - 1, layer), device_id_type=MESH)

    early = count // 2
    prev_order = [list(range(early)), list(range(early, count))]
    next_order = [list(range(early, count)), list(range(early))]

    def halo(part_of, act):
        @pl.when(me > 0)
        def _():
            for e in prev_order[part_of]:
                getattr(send_prev(e), act)()

        @pl.when(me < n_energy - 1)
        def _():
            for e in next_order[part_of]:
                getattr(send_next(e), act)()

    def halo_arrived(part_of):
        @pl.when(me < n_energy - 1)
        def _():
            for e in prev_order[part_of]:
                send_prev(e).wait_recv()

        @pl.when(me > 0)
        def _():
            for e in next_order[part_of]:
                send_next(e).wait_recv()

    halo(0, "start")

    @pl.when(me == 0)
    def _():
        for e in range(count):
            lo[e] = jnp.zeros(lo.shape[1:], lo.dtype)

    @pl.when(me == n_energy - 1)
    def _():
        for e in range(count):
            up[count + e] = jnp.zeros(up.shape[1:], up.dtype)

    def stage_own(e, carry):
        block = green_ref[e]
        lo[count + e] = block
        up[e] = block
        turned[count - early + e, 0] = block[0].T
        turned[count - early + e, 1] = block[1].T
        return carry

    lax.fori_loop(0, count, stage_own, 0)

    offs = [off_ref[k] for k in range(noff)]

    def first_of(value):
        found = jnp.int32(noff - 1)
        for k in range(noff - 2, -1, -1):
            found = jnp.where(offs[k] == value, jnp.int32(k), found)
        return found

    low_slot, high_slot = first_of(-count), first_of(count)
    slots = [low_slot, high_slot]
    last = jnp.int32(-1)
    for _ in range(noff - 2):
        found = jnp.int32(noff - 1)
        for k in range(noff - 1, -1, -1):
            fits = jnp.logical_and(jnp.logical_and(k != low_slot, k != high_slot), k > last)
            found = jnp.where(fits, jnp.int32(k), found)
        slots.append(found)
        last = found
    positive = []
    for s, k in enumerate(slots):
        w = off_ref[k]
        n = occ_ref[k]
        sign = jnp.where(w > 0, jnp.float32(1.0), jnp.float32(0.0))
        positive.append(sign)
        reach[s] = jnp.clip(jnp.where(w > 0, w, -w), 1, count)
        coef[s] = n + 1.0 - sign
        coef[noff + s] = n + sign
        v = coup_ref[0, k]
        real, imag = vertex_ref[v, 0], vertex_ref[v, 1]
        wide[s, 0:nb, 0:nb] = real
        wide[s, 0:nb, nb:2 * nb] = -imag
        wide[s, nb:2 * nb, 0:nb] = imag
        wide[s, nb:2 * nb, nb:2 * nb] = real
        real_t, imag_t = real.T, imag.T
        wide_t[s, 0:nb, 0:nb] = real_t
        wide_t[s, 0:nb, nb:2 * nb] = -imag_t
        wide_t[s, nb:2 * nb, 0:nb] = imag_t
        wide_t[s, nb:2 * nb, nb:2 * nb] = real_t

    def clear(i, carry):
        acc[i] = jnp.zeros(acc.shape[1:], F32)
        return carry

    lax.fori_loop(0, acc.shape[0], clear, 0)

    def place(bit):
        return layer if bit == 0 else lax.div(me, bit) % 2

    def region(s, m):
        start = jnp.int32(0)
        for pair, parts, split, size, after in plan[:s]:
            if split:
                start = start + place(pair[m % 2]) * after
        return start

    def rows_at(start, size):
        return pl.ds(pl.multiple_of(start, ALIGN), size)

    def target(bit, r):
        return (me, lax.rem(layer + r, n_layer)) if bit == 0 else (flipped(bit), layer)

    def sum_copy(s, m, r):
        pair, parts, split, size, after = plan[s]
        bit = pair[m % 2]
        start = region(s, m)
        if split:
            mine = lax.rem(layer + r, n_layer) if bit == 0 else 1 - place(bit)
            start = start + mine * after
        return pltpu.make_async_remote_copy(
            src_ref=part.at[m, rows_at(start, after)], dst_ref=landing[s].at[m, r - 1],
            send_sem=sums_send[s].at[m, r - 1], recv_sem=sums_recv[s].at[m, r - 1],
            device_id=target(bit, r), device_id_type=MESH)

    def spread_copy(s, m, r):
        pair, parts, split, size, after = plan[s]
        where = rows_at(region(s + 1, m), after)
        return pltpu.make_async_remote_copy(
            src_ref=full.at[m, where], dst_ref=full.at[m, where],
            send_sem=spread_send[s].at[m, r - 1], recv_sem=spread_recv[s].at[m, r - 1],
            device_id=target(pair[m % 2], r), device_id_type=MESH)

    steps = [(sum_copy, s) for s in range(stages)]
    steps += [(spread_copy, s) for s in range(stages - 1, -1, -1) if plan[s][2]]

    def begin(i, m):
        make, s = steps[i]
        for r in range(1, plan[s][1]):
            make(s, m, r).start()

    def finish(i, m):
        make, s = steps[i]
        pair, parts, split, size, after = plan[s]
        for r in range(1, parts):
            make(s, m, r).wait()
        if make is sum_copy:
            where = rows_at(region(s + 1, m), after)
            total = part[m, where].astype(F32)
            for r in range(1, parts):
                total = total + landing[s][m, r - 1].astype(F32)
            if s == stages - 1:
                full[m, where] = total.astype(BF16)
            else:
                part[m, where] = total.astype(BF16)

    halo(0, "wait_send")
    halo(1, "start")
    halo_arrived(0)
    for i in range(count - early):
        turned[i, 0] = lo[early + i, 0].T
        turned[i, 1] = lo[early + i, 1].T

    for q in range(nq):
        w = count if q == 0 else reach[q + 1]

        def polar_rows(i, carry, q=q, w=w):
            rows = pl.ds(pl.multiple_of(i * ROWS, ROWS), ROWS)
            real = jnp.zeros((ROWS, nb), F32)
            imag = jnp.zeros((ROWS, nb), F32)
            for f in range(early, count + early):
                b_real, b_imag = up[f, 0, rows], up[f, 1, rows]
                at = count - early + f - w
                if f > count and q > 0:
                    inside = w <= f - count
                    b_real = jnp.where(inside, up[f - count, 0, rows].astype(F32), b_real.astype(F32))
                    b_imag = jnp.where(inside, up[f - count, 1, rows].astype(F32), b_imag.astype(F32))
                    at = jnp.where(inside, at - count, at)
                b_real, b_imag = b_real.astype(F32), b_imag.astype(F32)
                a_real = turned[at, 0, rows].astype(F32)
                a_imag = turned[at, 1, rows].astype(F32)
                real = real + a_real * b_real - a_imag * b_imag
                imag = imag + a_real * b_imag + a_imag * b_real
            part[q, rows] = real.astype(BF16)
            part[q, pl.ds(pl.multiple_of(nb + i * ROWS, ROWS), ROWS)] = imag.astype(BF16)
            return carry

        lax.fori_loop(0, nb // ROWS, polar_rows, 0)
        begin(0, q)

    def advance(step):
        for m in range(nq):
            finish(step, m)
            if step + 1 < len(steps):
                begin(step + 1, m)

    ahead = min(AHEAD, len(steps))
    for step in range(ahead):
        advance(step)
    halo_arrived(1)

    pairs = count // 2
    units = noff * pairs

    def unit(i, carry):
        s, p = lax.div(i, pairs), lax.rem(i, pairs)
        w, c_low, c_up = reach[s], coef[s], coef[noff + s]

        def mix_rows(r, carry):
            rows = pl.ds(pl.multiple_of(r * ROWS, ROWS), ROWS)
            for j in range(2):
                e = 2 * p + j
                for c in range(2):
                    below = lo[count + e - w, c, rows].astype(F32)
                    above = up[e + w, c, rows].astype(F32)
                    to = pl.ds(pl.multiple_of(c * nb + r * ROWS, ROWS), ROWS)
                    mix[to, j * nb:(j + 1) * nb] = (c_low * below + c_up * above).astype(BF16)
            return carry

        lax.fori_loop(0, nb // ROWS, mix_rows, 0)
        for at in range(0, 2 * nb, WIDTH):
            product = jnp.dot(wide[s], mix[:, at:at + WIDTH], preferred_element_type=F32).astype(BF16)
            for g in range(at, at + WIDTH, LANES):
                j, col = g // nb, g % nb
                for c in range(2):
                    half[j * nb:(j + 1) * nb, c * nb + col:c * nb + col + LANES] = product[
                        c * nb:(c + 1) * nb, g - at:g - at + LANES]
        for at in range(0, 2 * nb, WIDTH):
            acc[p, :, at:at + WIDTH] += jnp.dot(
                half[...], wide_t[s, :, at:at + WIDTH], preferred_element_type=F32)
        for step in range(ahead, min(len(steps), ahead + units)):
            @pl.when(i == step - ahead)
            def _(step=step):
                advance(step)
        return carry

    lax.fori_loop(0, units, unit, 0)
    for step in range(ahead + units, len(steps)):
        advance(step)

    for s, k in enumerate(slots):
        f_real, f_imag = free_ref[k, 0], free_ref[k, 1]
        mix[0:nb, 0:nb] = f_real
        mix[0:nb, nb:2 * nb] = f_imag
        mix[nb:2 * nb, 0:nb] = -f_imag
        mix[nb:2 * nb, nb:2 * nb] = f_real
        q = 0 if s < 2 else s - 1
        for c in range(2):
            straight = full[q, c * nb:(c + 1) * nb]
            if s == 0:
                chosen = straight
            elif s == 1:
                chosen = straight.T
            else:
                flip = straight.T.astype(F32)
                chosen = (positive[s] * flip + (1.0 - positive[s]) * straight.astype(F32)).astype(BF16)
            half[0:nb, c * nb:(c + 1) * nb] = chosen
        magnon = jnp.dot(half[0:nb], mix[...], preferred_element_type=F32).astype(BF16).astype(F32)
        if s == 1:
            mag[0] += magnon
        else:
            mag[q] = magnon

    for e in range(count):
        def out_rows(i, carry, e=e):
            rows = pl.ds(pl.multiple_of(i * ROWS, ROWS), ROWS)
            base = pl.ds(pl.multiple_of((e % 2) * nb + i * ROWS, ROWS), ROWS)
            real = acc[e // 2, base, 0:nb]
            imag = acc[e // 2, base, nb:2 * nb]
            for q in range(nq):
                w = reach[0] if q == 0 else reach[q + 1]
                s_real = lo[count + e - w, 0, rows].astype(F32) + up[e + w, 0, rows].astype(F32)
                s_imag = lo[count + e - w, 1, rows].astype(F32) + up[e + w, 1, rows].astype(F32)
                m_real = mag[q, rows, 0:nb]
                m_imag = mag[q, rows, nb:2 * nb]
                real = real + m_real * s_real - m_imag * s_imag
                imag = imag + m_real * s_imag + m_imag * s_real
            out_ref[e, 0, 0, rows] = real.astype(BF16)
            out_ref[e, 0, 1, rows] = imag.astype(BF16)
            return carry

        lax.fori_loop(0, nb // ROWS, out_rows, 0)

    halo(1, "wait_send")


def per_device(n_energy, n_layer, green_blocks, offsets, occupation, coupling, vertex, magnon_free):
    count, _, _, nb, _ = green_blocks.shape
    noff = offsets.shape[0]
    nq = noff - 1
    plan = reduction_plan(n_energy, n_layer, 2 * nb)
    smem = pl.BlockSpec(memory_space=pltpu.SMEM)
    vmem = pl.BlockSpec(memory_space=pltpu.VMEM)
    dma = pltpu.SemaphoreType.DMA
    scratch = [
        pltpu.VMEM((2 * count, 2, nb, nb), BF16),
        pltpu.VMEM((2 * count, 2, nb, nb), BF16),
        pltpu.VMEM((2 * count - count // 2, 2, nb, nb), BF16),
        pltpu.VMEM((noff, 2 * nb, 2 * nb), BF16),
        pltpu.VMEM((noff, 2 * nb, 2 * nb), BF16),
        pltpu.VMEM((count // 2, 2 * nb, 2 * nb), F32),
        pltpu.VMEM((2 * nb, 2 * nb), BF16),
        pltpu.VMEM((2 * nb, 2 * nb), BF16),
        pltpu.VMEM((nq, 2 * nb, nb), BF16),
        pltpu.VMEM((nq, 2 * nb, nb), BF16),
        pltpu.VMEM((nq, nb, 2 * nb), F32),
        pltpu.SMEM((noff,), jnp.int32),
        pltpu.SMEM((2 * noff,), F32),
    ]
    scratch += [pltpu.VMEM((nq, parts - 1, after, nb), BF16) for _, parts, _, _, after in plan]
    scratch += [dma((2, count)), dma((2, count))]
    for _ in range(4):
        scratch += [dma((nq, parts - 1)) for _, parts, _, _, _ in plan]
    flops = 16 * count * noff * 2 * nb ** 3
    return pl.pallas_call(
        functools.partial(kernel, n_energy, n_layer, plan),
        out_shape=jax.ShapeDtypeStruct(green_blocks.shape, BF16),
        in_specs=[smem, smem, smem, vmem, vmem, vmem],
        out_specs=vmem,
        scratch_shapes=scratch,
        compiler_params=pltpu.CompilerParams(
            collective_id=0, has_side_effects=True, vmem_limit_bytes=60 * 1024 * 1024),
        cost_estimate=pl.CostEstimate(
            flops=flops, bytes_accessed=4 * green_blocks.size * 2, transcendentals=0),
    )(offsets, occupation, coupling, green_blocks.reshape(count, 2, nb, nb), vertex, magnon_free)


def solution(mesh):
    placed = (P("energy", "layer", None, None, None), P(), P(), P("layer", None), P(), P())
    return jax.shard_map(
        functools.partial(per_device, mesh.shape["energy"], mesh.shape["layer"]),
        mesh=mesh,
        in_specs=placed,
        out_specs=P("energy", "layer", None, None, None),
        check_vma=False,
    )
```
